32 devices in a mesh: groups: 1, stat: 32 (over z, y, x, core).
Axes of the slice: x: 2, y: 2, z: 4, core: 2. Of those that a mesh axis runs over, the one named last changes fastest.
Arguments:
- predicted_moments: bfloat16 [256, 65536], P(('groups', 'stat')), may hold values from -24 to 24
- member_vectors: bfloat16 [256, 32768], P(('groups', 'stat')), may hold values from -6 to 6
- measured_moments: float32 [65536], P(('groups', 'stat')), may hold values from -96 to 96
- block_error_group: int32 [128], P(('groups', 'stat')), may hold values from 0 to 23
- group_error_spread: float32 [24], P('groups'), may hold values from 0.08 to 64
- background_spread: float32 [1], P('groups'), may hold values from 11.313708 to 45.254833
- member_random_keys: int32 [256], P('groups'), may hold values from 0 to 16777215
Outputs:
- updated: bfloat16 [256, 32768], P(('groups', 'stat'))
- predicted: bfloat16 [256, 65536], P('groups', 'stat')
The draws below stay inside these ranges and needn't reach their ends.
All inputs are finite; a program needn't handle non-finite values.
Results may differ from the reference program's by a relative error of at most 0.008.
The reference program's roundings to bfloat16 on the way count: a program that leaves them out, or rounds other values in their place, can miss the bound.
Values may be sent and summed in bfloat16 or wider, within the bound.
A program may use at most 64 MiB of HBM per device.

```python
import math
import jax
import jax.numpy as jnp
from jax import lax

J = 256
MOMENTS_EACH_KEY = 2048
PAR_DEV = 1024
SLAB = 512
NCLASS = 24
M = 65536
P_SIZE = 32768
NSLAB = 128
N_STAT = 32


def shared_draws(key):
    pieces = jax.random.split(key, 5)
    classes = jax.random.randint(pieces[0], (NSLAB,), 0, NCLASS, dtype=jnp.int32)
    levels = jax.random.uniform(pieces[1], (NCLASS,), jnp.float32)
    ranking = jax.random.permutation(pieces[2], NCLASS)
    common = jax.random.uniform(pieces[3], (M,), jnp.float32, -1.0, 1.0)
    deviates = jax.random.uniform(pieces[4], (M,), jnp.float32, -1.7320508, 1.7320508)
    return (classes, levels, ranking, common, deviates)


def class_spread(levels, ranking, quiet_count, quiet_low, quiet_high):
    root_scale = (M // J) ** 0.5
    drawn_spread = jnp.exp(math.log(0.25) + levels * math.log(16.0))
    quiet_spread = jnp.exp(math.log(quiet_low) + levels * math.log(quiet_high / quiet_low))
    quiet_mask = ranking < quiet_count
    return jnp.where(quiet_mask, quiet_spread, drawn_spread) * root_scale


def draw_block_error_group(key, part):
    drawn = shared_draws(key)
    return drawn[0]


def draw_group_error_spread(key, part):
    drawn = shared_draws(key)
    return class_spread(drawn[1], drawn[2], 0, 0.005, 0.01)


def draw_measured_moments(key, part):
    key = jax.random.fold_in(key, 9)
    root_scale = (M // J) ** 0.5
    values = root_scale * jax.random.normal(key, (M,), jnp.float32)
    return jnp.clip(values, -6.0 * root_scale, 6.0 * root_scale)


def draw_predicted_moments(key, part):
    key = jax.random.fold_in(key, 7)
    subkeys = jax.random.split(key, 4)
    pairing = jax.random.permutation(subkeys[0], J)
    jitter = jax.random.normal(subkeys[1], (J, M), jnp.float32)
    members = jitter + 0.7 * jitter[pairing, :]
    common = 2.0 * jax.random.normal(subkeys[3], (M,), jnp.float32)
    return jnp.clip(common[None, :] + members, -24.0, 24.0).astype(jnp.bfloat16)


def place_ends(entries, own_key, least, high):
    extent = entries.shape
    spot = [jax.random.randint(jax.random.fold_in(own_key, axis), (), 0, extent[axis]) for axis in range(len(extent))]
    entries = entries.at[tuple(spot)].set(least)
    longest = extent.index(max(extent))
    spot[longest] = (spot[longest] + 1) % extent[longest]
    return entries.at[tuple(spot)].set(high)


def steps_of(rng, dims, shards, smallest, top_value):
    def one(dim, parts):
        draws = jax.random.uniform(jax.random.fold_in(jax.random.fold_in(rng, 6), dim), (parts,), jnp.float32, smallest / len(shards), top_value / len(shards))
        return jnp.repeat(jnp.exp(draws), dims[dim] // parts).reshape((-1,) + (1,) * (len(dims) - dim - 1))

    loudness = one(*shards[0])
    for cut in shards[1:]:
        loudness = loudness * one(*cut)
    return loudness


def scatter_about(rng, shape, scale, most, cuts=(), kind=jnp.bfloat16):
    values = jax.random.normal(rng, shape, jnp.float32) * scale
    if len(cuts) > 0:
        values = steps_of(rng, shape, cuts, -0.22, 0.18) * values
    return jnp.clip(values, min=-most, max=most).astype(kind)


def setup_inputs(seed: int = 0, part: int = 0) -> dict:
    seeds = jax.random.split(jax.random.key(seed), 8)
    own_keys = jax.random.split(jax.random.fold_in(seeds[7], part), 8)
    return {
        "predicted_moments": draw_predicted_moments(jax.random.fold_in(jax.random.fold_in(seeds[7], part), 71), part),
        "member_vectors": scatter_about(own_keys[1], (J, P_SIZE), 1.0, 6.0, ((0, 32),)),
        "measured_moments": draw_measured_moments(jax.random.fold_in(jax.random.fold_in(seeds[7], part), 71), part),
        "block_error_group": draw_block_error_group(jax.random.fold_in(jax.random.fold_in(seeds[7], part), 71), part),
        "group_error_spread": draw_group_error_spread(jax.random.fold_in(jax.random.fold_in(seeds[7], part), 71), part),
        "background_spread": jnp.clip(jnp.exp(jax.random.uniform(own_keys[5], (1,), jnp.float32, math.log(11.313708), math.log(45.254833))), 11.313708, 45.254833),
        "member_random_keys": place_ends(jax.random.randint(own_keys[6], (J,), 0, 16777216), jax.random.fold_in(own_keys[6], 1), 0, 16777215).astype(jnp.int32),
    }


seed_factor = 668265261
index_factor = 374761393
scramble_one = 2146121005
scramble_two = 739982445

def scramble(hashed):
    hashed = hashed ^ lax.shift_right_logical(hashed, jnp.int32(16))
    hashed = hashed * scramble_one
    hashed = hashed ^ lax.shift_right_logical(hashed, jnp.int32(15))
    hashed = hashed * scramble_two
    return hashed ^ lax.shift_right_logical(hashed, jnp.int32(16))

def uniform_from(hashed):
    quotient = lax.shift_right_logical(scramble(hashed), jnp.int32(9))
    return (quotient.astype(jnp.float32) + 0.5) * 2.0 ** (-23)

def normal_draw(member_random_keys, position):
    hashed = member_random_keys[:, None] * seed_factor + position[None, :] * index_factor
    first_part = uniform_from(hashed)
    second_part = uniform_from(hashed + 1)
    return jnp.sqrt(-2.0 * jnp.log(first_part)) * jnp.cos(2.0 * math.pi * second_part)

def inner(left, right):
    return lax.dot_general(left.astype(jnp.float32), right.astype(jnp.float32), (((1,), (1,)), ((), ())), preferred_element_type=jnp.float32)

def transposed_product(weights, right):
    return lax.dot_general(weights.astype(jnp.float32), right.astype(jnp.float32), (((0,), (0,)), ((), ())), preferred_element_type=jnp.float32)

def solve_system(gram, right):
    system = jnp.eye(gram.shape[0], dtype=jnp.float32) + gram
    factor = jnp.linalg.cholesky(system)
    middle = lax.linalg.triangular_solve(factor, right, left_side=True, lower=True)
    return lax.linalg.triangular_solve(factor, middle, left_side=True, lower=True, transpose_a=True)

def reference(predicted_moments, member_vectors, measured_moments, block_error_group, group_error_spread, background_spread, member_random_keys):
    root_scale = math.sqrt(J - 1.0)
    prior = background_spread[0]
    sigma = jnp.repeat(group_error_spread[block_error_group], SLAB)
    stat_offsets = jnp.arange(N_STAT, dtype=jnp.int32) * MOMENTS_EACH_KEY
    par_offsets = jnp.arange(N_STAT, dtype=jnp.int32) * PAR_DEV

    def stat_pieces(first_position):
        closure_results = lax.dynamic_slice_in_dim(predicted_moments, first_position, MOMENTS_EACH_KEY, 1).astype(jnp.float32)
        scales = lax.dynamic_slice_in_dim(sigma, first_position, MOMENTS_EACH_KEY, 0)
        observed = lax.dynamic_slice_in_dim(measured_moments, first_position, MOMENTS_EACH_KEY, 0)
        average = lax.optimization_barrier(jnp.mean(closure_results, axis=0))
        anomaly = ((closure_results - average) / (scales * root_scale)).astype(jnp.bfloat16)
        position = first_position + jnp.arange(MOMENTS_EACH_KEY, dtype=jnp.int32)
        misfit = ((observed - closure_results) / scales + normal_draw(member_random_keys, position)).astype(jnp.bfloat16)
        return (closure_results, scales, anomaly, misfit)

    def par_pieces(first_position):
        params = lax.dynamic_slice_in_dim(member_vectors, first_position, PAR_DEV, 1).astype(jnp.float32)
        average = lax.optimization_barrier(jnp.mean(params, axis=0))
        spread = ((params - average) / root_scale).astype(jnp.bfloat16)
        position = M + first_position + jnp.arange(PAR_DEV, dtype=jnp.int32)
        misfit = (-params / prior + normal_draw(member_random_keys, position)).astype(jnp.bfloat16)
        return (params, spread, misfit)

    def add_stat(carry, first_position):
        pieces = stat_pieces(first_position)
        return ((carry[0] + inner(pieces[2], pieces[2]), carry[1] + inner(pieces[2], pieces[3])), None)

    def add_par(carry, first_position):
        pieces = par_pieces(first_position)
        gram_term = inner(pieces[1], pieces[1]) / (prior * prior)
        cross_term = inner(pieces[1], pieces[2]) / prior
        return ((carry[0] + gram_term, carry[1] + cross_term), None)
    zeros = jnp.zeros((J, J), jnp.float32)
    totals = lax.scan(add_stat, (zeros, zeros), stat_offsets)[0]
    totals = lax.scan(add_par, totals, par_offsets)[0]
    weights = solve_system(totals[0], totals[1]).astype(jnp.bfloat16)

    def new_params(first_position):
        pieces = par_pieces(first_position)
        return (pieces[0] + transposed_product(weights, pieces[1])).astype(jnp.bfloat16)

    def new_outputs(first_position):
        pieces = stat_pieces(first_position)
        return (pieces[0] + pieces[1][None, :] * transposed_product(weights, pieces[2])).astype(jnp.bfloat16)
    updated = jnp.transpose(lax.map(new_params, par_offsets), (1, 0, 2)).reshape(J, P_SIZE)
    predicted = jnp.transpose(lax.map(new_outputs, stat_offsets), (1, 0, 2)).reshape(J, M)
    return (updated, predicted)
```

```python
import functools
import math

import jax
import jax.numpy as jnp
from jax import lax
from jax.experimental import pallas as pl
from jax.experimental.pallas import tpu as pltpu
from jax.sharding import PartitionSpec as P

SLAB = 512
LANES = 128
BLOCK = 16
MESH = pl.DeviceIdType.MESH

seed_factor = 668265261
index_factor = 374761393
scramble_one = 2146121005
scramble_two = 739982445


def scramble(hashed):
    hashed = hashed ^ lax.shift_right_logical(hashed, jnp.int32(16))
    hashed = hashed * scramble_one
    hashed = hashed ^ lax.shift_right_logical(hashed, jnp.int32(15))
    hashed = hashed * scramble_two
    return hashed ^ lax.shift_right_logical(hashed, jnp.int32(16))


def uniform_from(hashed):
    quotient = lax.shift_right_logical(scramble(hashed), jnp.int32(9))
    return (quotient.astype(jnp.float32) + 0.5) * 2.0 ** (-23)


def normal_draw(member_random_keys, position):
    hashed = member_random_keys[:, None] * seed_factor + position[None, :] * index_factor
    first_part = uniform_from(hashed)
    second_part = uniform_from(hashed + 1)
    return jnp.sqrt(-2.0 * jnp.log(first_part)) * jnp.cos(2.0 * math.pi * second_part)


def inner(left, right):
    return lax.dot_general(
        left, right, (((1,), (1,)), ((), ())), preferred_element_type=jnp.float32
    )


def transposed_product(weights, right):
    return lax.dot_general(
        weights, right, (((0,), (0,)), ((), ())), preferred_element_type=jnp.float32
    )


def stages_of(mesh_size):
    rest = mesh_size // 2
    second = 1
    while second * second < rest:
        second *= 2
    return ((1, 2), (2, second), (2 * second, rest // second))


def sum_kernel(stages, x_ref, o_ref, *scratch):
    count = len(stages)
    recvs = scratch[:count]
    totals = scratch[count : 2 * count]
    gathered, send_sem, recv_sem, gsend_sem, grecv_sem = scratch[2 * count :]
    me = lax.axis_index("stat")
    digits = [lax.rem(lax.div(me, stride), size) for stride, size in stages]

    def peer(t, offset):
        stride, size = stages[t]
        other = lax.rem(digits[t] + offset, size)
        return other, me + (other - digits[t]) * stride

    barrier = pltpu.get_barrier_semaphore()
    peers = 0
    for t, (stride, size) in enumerate(stages):
        for offset in range(1, size):
            pl.semaphore_signal(
                barrier, inc=1, device_id={"stat": peer(t, offset)[1]}, device_id_type=MESH
            )
            peers += 1
    pl.semaphore_wait(barrier, peers)

    source = x_ref
    length = x_ref.shape[0]
    bases = [0]
    slot = 0
    for t, (stride, size) in enumerate(stages):
        piece = length // size
        copies = []
        for offset in range(1, size):
            other, device = peer(t, offset)
            copy = pltpu.make_async_remote_copy(
                src_ref=source.at[pl.ds(other * piece, piece)],
                dst_ref=recvs[t].at[offset - 1],
                send_sem=send_sem.at[slot],
                recv_sem=recv_sem.at[slot],
                device_id={"stat": device},
                device_id_type=MESH,
            )
            copy.start()
            copies.append(copy)
            slot += 1
        value = source[pl.ds(digits[t] * piece, piece)]
        for offset in range(1, size):
            copies[offset - 1].wait_recv()
            value = value + recvs[t][offset - 1]
        totals[t][...] = value
        for copy in copies:
            copy.wait_send()
        bases.append(bases[t] + digits[t] * piece)
        source, length = totals[t], piece

    gathered[pl.ds(bases[count], length)] = source[...]
    slot = 0
    for t in reversed(range(count)):
        stride, size = stages[t]
        copies = []
        for offset in range(1, size):
            _, device = peer(t, offset)
            own = gathered.at[pl.ds(bases[t + 1], length)]
            copy = pltpu.make_async_remote_copy(
                src_ref=own,
                dst_ref=own,
                send_sem=gsend_sem.at[slot],
                recv_sem=grecv_sem.at[slot],
                device_id={"stat": device},
                device_id_type=MESH,
            )
            copy.start()
            copies.append(copy)
            slot += 1
        for copy in copies:
            copy.wait()
        length *= size
    o_ref[...] = gathered[...]


def sum_over_devices(part, devices_total):
    rows, columns = part.shape
    chunks = max(rows // 8, devices_total)
    spread = chunks // (rows // 8)
    width = columns // spread
    packed = part.reshape(rows // 8, 8, spread, width).transpose(0, 2, 1, 3)
    packed = packed.reshape(chunks, 8, width)
    stages = stages_of(devices_total)
    recvs, totals, length, copies = [], [], chunks, 0
    for stride, size in stages:
        length //= size
        recvs.append(pltpu.VMEM((size - 1, length, 8, width), jnp.float32))
        totals.append(pltpu.VMEM((length, 8, width), jnp.float32))
        copies += size - 1
    whole = pl.BlockSpec(memory_space=pltpu.VMEM)
    out = pl.pallas_call(
        functools.partial(sum_kernel, stages),
        out_shape=jax.ShapeDtypeStruct(packed.shape, jnp.float32),
        in_specs=[whole],
        out_specs=whole,
        scratch_shapes=recvs
        + totals
        + [pltpu.VMEM(packed.shape, jnp.float32)]
        + [pltpu.SemaphoreType.DMA((copies,))] * 4,
        compiler_params=pltpu.CompilerParams(
            collective_id=0, has_side_effects=True, vmem_limit_bytes=16 * 2**20
        ),
        name="sum_over_devices",
    )(packed)
    return out.reshape(rows // 8, spread, 8, width).transpose(0, 2, 1, 3).reshape(rows, columns)


def exact_dot(left, right):
    return jnp.dot(
        left, right, preferred_element_type=jnp.float32, precision=lax.Precision.HIGHEST
    )


def solve_kernel(s_ref, w_ref, m_ref):
    size = s_ref.shape[0]
    groups = s_ref.shape[1] // LANES
    own = size // LANES
    row = lax.broadcasted_iota(jnp.int32, (size, size), 0)
    column = lax.broadcasted_iota(jnp.int32, (size, size), 1)
    m_ref[:, :size] = s_ref[:, :size] + (row == column).astype(jnp.float32)
    m_ref[:, size:] = s_ref[:, size:]
    row_id = lax.broadcasted_iota(jnp.int32, (BLOCK, LANES), 0)
    for start in range(0, size, BLOCK):
        group = start // LANES
        lane = start % LANES
        panel = [
            m_ref[start : start + BLOCK, g * LANES : (g + 1) * LANES]
            for g in range(group, groups)
        ]
        head = panel[0]
        splat = [
            jnp.broadcast_to(head[:, lane + j : lane + j + 1], (BLOCK, LANES))
            for j in range(BLOCK)
        ]
        for j in range(BLOCK):
            inverse = 1.0 / splat[j][j : j + 1, :]
            at_pivot = row_id == j
            factor = splat[j]

            def step(block):
                scaled = block[j : j + 1, :] * inverse
                return jnp.where(at_pivot, scaled, block - factor * scaled)

            for later in range(j + 1, BLOCK):
                splat[later] = step(splat[later])
            panel = [step(block) for block in panel]
        top = jnp.concatenate(panel, axis=1)
        pieces = []
        if lane > 0:
            pieces.append(jnp.zeros((lane, top.shape[1]), jnp.float32))
        pieces.append(top)
        if lane + BLOCK < LANES:
            pieces.append(jnp.zeros((LANES - lane - BLOCK, top.shape[1]), jnp.float32))
        right = jnp.concatenate(pieces, axis=0)
        left = m_ref[:, group * LANES : (group + 1) * LANES]
        from_column = group * LANES
        after = start + BLOCK
        spans = []
        if after < size:
            spans.append((after, after + BLOCK))
            if after + BLOCK < size:
                spans.append((after + BLOCK, size))
        if start > 0:
            spans.append((0, start))
        for low, high in spans:
            m_ref[low:high, from_column:] = m_ref[low:high, from_column:] - exact_dot(
                left[low:high], right
            )
        m_ref[start:after, from_column:] = top
    w_ref[...] = m_ref[:, size:].astype(w_ref.dtype)


def solve_system(total):
    size = total.shape[0]
    whole = pl.BlockSpec(memory_space=pltpu.VMEM)
    return pl.pallas_call(
        solve_kernel,
        out_shape=jax.ShapeDtypeStruct((size, total.shape[1] - size), jnp.bfloat16),
        in_specs=[whole],
        out_specs=whole,
        scratch_shapes=[pltpu.VMEM(total.shape, jnp.float32)],
        compiler_params=pltpu.CompilerParams(vmem_limit_bytes=16 * 2**20),
        name="solve_system",
    )(total)


def body(
    predicted_moments,
    member_vectors,
    measured_moments,
    block_error_group,
    group_error_spread,
    background_spread,
    member_random_keys,
):
    devices_total = lax.axis_size("stat")
    device_rank = lax.axis_index("stat")
    stat_width = measured_moments.shape[0]
    par_width = member_vectors.shape[1] // devices_total
    members = member_random_keys.shape[0]
    root_scale = math.sqrt(members - 1.0)
    prior = background_spread[0]
    shard_result_lines = lax.all_to_all(
        predicted_moments, "stat", split_axis=1, concat_axis=0, tiled=True
    )
    params_rows = lax.all_to_all(member_vectors, "stat", split_axis=1, concat_axis=0, tiled=True)
    classes = group_error_spread.shape[0]
    selector = (block_error_group[:, None] == jnp.arange(classes, dtype=jnp.int32)[None, :]).astype(
        jnp.float32
    )
    slab_sigma = jnp.dot(selector, group_error_spread, precision=lax.Precision.HIGHEST)
    sigma = jnp.broadcast_to(slab_sigma[:, None], (block_error_group.shape[0], SLAB)).reshape(
        stat_width
    )
    closure_results = shard_result_lines.astype(jnp.float32)
    out_average = jnp.mean(closure_results, axis=0)
    anomaly = ((closure_results - out_average) / (sigma * root_scale)).astype(jnp.bfloat16)
    stat_position = device_rank * stat_width + jnp.arange(stat_width, dtype=jnp.int32)
    misfit = (
        (measured_moments - closure_results) / sigma
        + normal_draw(member_random_keys, stat_position)
    ).astype(jnp.bfloat16)
    params = params_rows.astype(jnp.float32)
    par_average = jnp.mean(params, axis=0)
    spread = ((params - par_average) / root_scale).astype(jnp.bfloat16)
    par_position = (
        devices_total * stat_width
        + device_rank * par_width
        + jnp.arange(par_width, dtype=jnp.int32)
    )
    prior_misfit = (-params / prior + normal_draw(member_random_keys, par_position)).astype(
        jnp.bfloat16
    )
    gram_part = inner(anomaly, anomaly) + inner(spread, spread) / (prior * prior)
    cross_part = inner(anomaly, misfit) + inner(spread, prior_misfit) / prior
    total = sum_over_devices(jnp.concatenate([gram_part, cross_part], axis=1), devices_total)
    weights = solve_system(total)
    updated_rows = (params + transposed_product(weights, spread)).astype(jnp.bfloat16)
    updated = lax.all_to_all(updated_rows, "stat", split_axis=0, concat_axis=1, tiled=True)
    predicted = (closure_results + sigma[None, :] * transposed_product(weights, anomaly)).astype(
        jnp.bfloat16
    )
    return (updated, predicted)


def solution(mesh):
    placed = (
        P(("groups", "stat"), None),
        P(("groups", "stat"), None),
        P(("groups", "stat")),
        P(("groups", "stat")),
        P("groups"),
        P("groups"),
        P("groups"),
    )
    return jax.shard_map(
        body,
        mesh=mesh,
        in_specs=placed,
        out_specs=(P(("groups", "stat"), None), P("groups", "stat")),
        check_vma=False,
    )
```

```python
import functools
import math

import jax
import jax.numpy as jnp
from jax import lax
from jax.experimental import pallas as pl
from jax.experimental.pallas import tpu as pltpu
from jax.sharding import PartitionSpec as P

SLAB = 512
LANES = 128
BLOCK = 16
MESH = pl.DeviceIdType.MESH

seed_factor = 668265261
index_factor = 374761393
scramble_one = 2146121005
scramble_two = 739982445


def scramble(hashed):
    hashed = hashed ^ lax.shift_right_logical(hashed, jnp.int32(16))
    hashed = hashed * scramble_one
    hashed = hashed ^ lax.shift_right_logical(hashed, jnp.int32(15))
    hashed = hashed * scramble_two
    return hashed ^ lax.shift_right_logical(hashed, jnp.int32(16))


def uniform_from(hashed):
    quotient = lax.shift_right_logical(scramble(hashed), jnp.int32(9))
    return (quotient.astype(jnp.float32) + 0.5) * 2.0 ** (-23)


def sine_of_turns(turns):
    square = turns * turns
    value = jnp.float32(0.0)
    for power in (11, 9, 7, 5, 3, 1):
        sign = -1.0 if power % 4 == 3 else 1.0
        value = value * square + sign * (2.0 * math.pi) ** power / math.factorial(power)
    return value * turns


def normal_from(hashed):
    first_part = uniform_from(hashed)
    second_part = uniform_from(hashed + 1)
    radius = jnp.sqrt(jnp.maximum(-2.0 * jnp.log(first_part), 0.0))
    return radius * sine_of_turns(jnp.abs(second_part - 0.5) - 0.25)


def inner(left, right):
    return lax.dot_general(
        left, right, (((1,), (1,)), ((), ())), preferred_element_type=jnp.float32
    )


def transposed_product(weights, right):
    return lax.dot_general(
        weights, right, (((0,), (0,)), ((), ())), preferred_element_type=jnp.float32
    )


def stages_of(mesh_size):
    rest = mesh_size // 2
    second = 1
    while second * second < rest:
        second *= 2
    return ((1, 2), (2, second), (2 * second, rest // second))


def signal_peers(barrier, me, devices_total):
    def signal(offset, carry):
        pl.semaphore_signal(
            barrier,
            inc=1,
            device_id={"stat": lax.rem(me + offset, devices_total)},
            device_id_type=MESH,
        )
        return carry

    lax.fori_loop(1, devices_total, signal, 0)
    pl.semaphore_wait(barrier, devices_total - 1)


def sum_stages(stages, me, x_ref, recvs, totals, gathered, send_sem, recv_sem, gsend_sem, grecv_sem):
    count = len(stages)
    digits = [lax.rem(lax.div(me, stride), size) for stride, size in stages]

    def peer(t, offset):
        stride, size = stages[t]
        other = lax.rem(digits[t] + offset, size)
        return other, me + (other - digits[t]) * stride

    source = x_ref
    length = x_ref.shape[0]
    bases = [0]
    slot = 0
    for t, (stride, size) in enumerate(stages):
        piece = length // size
        copies = []
        for offset in range(1, size):
            other, device = peer(t, offset)
            copy = pltpu.make_async_remote_copy(
                src_ref=source.at[pl.ds(other * piece, piece)],
                dst_ref=recvs[t].at[offset - 1],
                send_sem=send_sem.at[slot],
                recv_sem=recv_sem.at[slot],
                device_id={"stat": device},
                device_id_type=MESH,
            )
            copy.start()
            copies.append(copy)
            slot += 1
        value = source[pl.ds(digits[t] * piece, piece)]
        for offset in range(1, size):
            copies[offset - 1].wait_recv()
            value = value + recvs[t][offset - 1]
        totals[t][...] = value
        for copy in copies:
            copy.wait_send()
        bases.append(bases[t] + digits[t] * piece)
        source, length = totals[t], piece

    gathered[pl.ds(bases[count], length)] = source[...]
    slot = 0
    for t in reversed(range(count)):
        stride, size = stages[t]
        copies = []
        for offset in range(1, size):
            _, device = peer(t, offset)
            own = gathered.at[pl.ds(bases[t + 1], length)]
            copy = pltpu.make_async_remote_copy(
                src_ref=own,
                dst_ref=own,
                send_sem=gsend_sem.at[slot],
                recv_sem=grecv_sem.at[slot],
                device_id={"stat": device},
                device_id_type=MESH,
            )
            copy.start()
            copies.append(copy)
            slot += 1
        for copy in copies:
            copy.wait()
        length *= size


DRAW_ROWS = 8
DRAW_LANES = 1024
MIX = 13


def exchange_kernel(
    stages,
    devices_total,
    group_ref,
    spread_of_group_ref,
    prior_ref,
    keys_ref,
    measured_ref,
    moments_ref,
    vectors_ref,
    total_ref,
    closure_ref,
    anomaly_ref,
    params_ref,
    spread_ref,
    got_moments,
    got_vectors,
    draws,
    part,
    packed,
    send_sem,
    recv_sem,
    own_sem,
    *sum_scratch,
):
    me = lax.axis_index("stat")
    members, stat_width = closure_ref.shape
    par_width = params_ref.shape[1]
    root_scale = math.sqrt(members - 1.0)
    barrier = pltpu.get_barrier_semaphore()
    signal_peers(barrier, me, devices_total)

    def columns(device, width):
        return pl.ds(pl.multiple_of(device * width, width), width)

    kinds = ((moments_ref, got_moments, stat_width), (vectors_ref, got_vectors, par_width))

    def copy_to(kind, step):
        source, slots, width = kinds[kind]
        device = lax.rem(me + lax.rem(step * MIX, devices_total), devices_total)
        return pltpu.make_async_remote_copy(
            src_ref=source.at[:, columns(device, width)],
            dst_ref=slots.at[me],
            send_sem=send_sem.at[kind, step],
            recv_sem=recv_sem.at[kind, step],
            device_id={"stat": device},
            device_id_type=MESH,
        )

    def copy_from(kind, step):
        source, slots, width = kinds[kind]
        device = lax.rem(
            me + devices_total - lax.rem(step * MIX, devices_total), devices_total
        )
        return pltpu.make_async_remote_copy(
            src_ref=source.at[:, columns(me, width)],
            dst_ref=slots.at[device],
            send_sem=send_sem.at[kind, step],
            recv_sem=recv_sem.at[kind, step],
            device_id={"stat": device},
            device_id_type=MESH,
        )

    own = []
    for kind, (source, slots, width) in enumerate(kinds):

        def start(step, carry, kind=kind):
            copy_to(kind, step).start()
            return carry

        lax.fori_loop(1, devices_total, start, 0)
        copy = pltpu.make_async_copy(
            source.at[:, columns(me, width)], slots.at[me], own_sem.at[kind]
        )
        copy.start()
        own.append(copy)

    def wait_kind(kind):
        def wait(step, carry):
            copy_from(kind, step).wait_recv()
            return carry

        lax.fori_loop(1, devices_total, wait, 0)
        own[kind].wait()

    lane = lax.broadcasted_iota(jnp.int32, (DRAW_ROWS, DRAW_LANES), 1)
    for first in range(0, stat_width + par_width, DRAW_LANES):
        if first < stat_width:
            position = me * stat_width + first
        else:
            position = devices_total * stat_width + me * par_width + (first - stat_width)
        offsets = (lane + position) * index_factor

        def draw(block, carry, first=first, offsets=offsets):
            rows = pl.ds(pl.multiple_of(block * DRAW_ROWS, DRAW_ROWS), DRAW_ROWS)
            hashed = keys_ref[rows, :] * seed_factor + offsets
            draws[rows, first : first + DRAW_LANES] = normal_from(hashed)
            return carry

        lax.fori_loop(0, members // DRAW_ROWS, draw, 0)

    wait_kind(0)
    for slab in range(stat_width // SLAB):
        here = slice(slab * SLAB, (slab + 1) * SLAB)
        raw = got_moments[:, :, here].astype(jnp.float32).reshape(members, SLAB)
        closure_ref[:, here] = raw.astype(jnp.bfloat16)
        sigma = jnp.full((1, SLAB), spread_of_group_ref[group_ref[slab]], jnp.float32)
        average = jnp.sum(raw, axis=0, keepdims=True) * (1.0 / members)
        anomaly = ((raw - average) * (1.0 / (sigma * root_scale))).astype(jnp.bfloat16)
        anomaly_ref[:, here] = anomaly
        misfit = (
            (measured_ref[:, here] - raw) * (1.0 / sigma) + draws[:, here]
        ).astype(jnp.bfloat16)
        product = inner(anomaly, jnp.concatenate([anomaly, misfit], axis=0))
        part[...] = product if slab == 0 else part[...] + product

    wait_kind(1)
    prior = jnp.full((1, SLAB), prior_ref[0], jnp.float32)
    prior_inverse = 1.0 / prior
    lanes = lax.broadcasted_iota(jnp.int32, (1, 2 * members), 1)
    prior_members = jnp.full((1, 2 * members), prior_ref[0], jnp.float32)
    scale = 1.0 / jnp.where(lanes < members, prior_members * prior_members, prior_members)
    for slab in range(par_width // SLAB):
        here = slice(slab * SLAB, (slab + 1) * SLAB)
        raw = got_vectors[:, :, here].astype(jnp.float32).reshape(members, SLAB)
        params_ref[:, here] = raw.astype(jnp.bfloat16)
        average = jnp.sum(raw, axis=0, keepdims=True) * (1.0 / members)
        spread = ((raw - average) * (1.0 / root_scale)).astype(jnp.bfloat16)
        spread_ref[:, here] = spread
        drawn = draws[:, stat_width + slab * SLAB : stat_width + (slab + 1) * SLAB]
        misfit = (drawn - raw * prior_inverse).astype(jnp.bfloat16)
        product = inner(spread, jnp.concatenate([spread, misfit], axis=0))
        part[...] += product * scale

    chunks, _, width = packed.shape
    fold = (2 * members) // width
    if fold == 1:
        packed[...] = part[...].reshape(packed.shape)
    else:
        for chunk in range(chunks):
            low, side = chunk // fold * 8, chunk % fold * width
            packed[chunk] = part[low : low + 8, side : side + width]
    gathered = sum_scratch[2 * len(stages)]
    sum_stages(
        stages,
        me,
        packed,
        sum_scratch[: len(stages)],
        sum_scratch[len(stages) : 2 * len(stages)],
        gathered,
        *sum_scratch[2 * len(stages) + 1 :],
    )
    if fold == 1:
        total_ref[...] = gathered[...].reshape(total_ref.shape)
    else:
        for chunk in range(chunks):
            low, side = chunk // fold * 8, chunk % fold * width
            total_ref[low : low + 8, side : side + width] = gathered[chunk]

    def wait_sent(step, carry):
        copy_to(0, step).wait_send()
        copy_to(1, step).wait_send()
        return carry

    lax.fori_loop(1, devices_total, wait_sent, 0)


def exchange(
    predicted_moments,
    member_vectors,
    measured_moments,
    block_error_group,
    group_error_spread,
    background_spread,
    member_random_keys,
    devices_total,
):
    each, all_moments = predicted_moments.shape
    stat_width = all_moments // devices_total
    par_width = member_vectors.shape[1] // devices_total
    members = each * devices_total
    chunks = max(members // 8, devices_total)
    packed = (chunks, 8, members // 8 * 2 * members // chunks)
    stages = stages_of(devices_total)
    recvs, totals, length, copies = [], [], chunks, 0
    for stride, size in stages:
        length //= size
        recvs.append(pltpu.VMEM((size - 1, length) + packed[1:], jnp.float32))
        totals.append(pltpu.VMEM((length,) + packed[1:], jnp.float32))
        copies += size - 1
    vmem = pl.BlockSpec(memory_space=pltpu.VMEM)
    smem = pl.BlockSpec(memory_space=pltpu.SMEM)
    anywhere = pl.BlockSpec(memory_space=pl.ANY)
    shape = jax.ShapeDtypeStruct
    return pl.pallas_call(
        functools.partial(exchange_kernel, stages, devices_total),
        out_shape=(
            shape((members, 2 * members), jnp.float32),
            shape((members, stat_width), jnp.bfloat16),
            shape((members, stat_width), jnp.bfloat16),
            shape((members, par_width), jnp.bfloat16),
            shape((members, par_width), jnp.bfloat16),
        ),
        in_specs=[smem, smem, smem, vmem, vmem, anywhere, anywhere],
        out_specs=(vmem,) * 5,
        scratch_shapes=[
            pltpu.VMEM((devices_total, each, stat_width), jnp.bfloat16),
            pltpu.VMEM((devices_total, each, par_width), jnp.bfloat16),
            pltpu.VMEM((members, stat_width + par_width), jnp.float32),
            pltpu.VMEM((members, 2 * members), jnp.float32),
            pltpu.VMEM(packed, jnp.float32),
            pltpu.SemaphoreType.DMA((2, devices_total)),
            pltpu.SemaphoreType.DMA((2, devices_total)),
            pltpu.SemaphoreType.DMA((2,)),
        ]
        + recvs
        + totals
        + [pltpu.VMEM(packed, jnp.float32)]
        + [pltpu.SemaphoreType.DMA((copies,))] * 4,
        compiler_params=pltpu.CompilerParams(
            collective_id=0, has_side_effects=True, vmem_limit_bytes=40 * 2**20
        ),
        name="exchange",
    )(
        block_error_group,
        group_error_spread,
        background_spread,
        member_random_keys[:, None],
        measured_moments[None, :],
        predicted_moments,
        member_vectors,
    )


def exact_dot(left, right):
    return jnp.dot(
        left, right, preferred_element_type=jnp.float32, precision=lax.Precision.HIGHEST
    )


def solve_kernel(s_ref, w_ref, m_ref):
    size = s_ref.shape[0]
    groups = s_ref.shape[1] // LANES
    own = size // LANES
    row = lax.broadcasted_iota(jnp.int32, (size, size), 0)
    column = lax.broadcasted_iota(jnp.int32, (size, size), 1)
    m_ref[:, :size] = s_ref[:, :size] + (row == column).astype(jnp.float32)
    m_ref[:, size:] = s_ref[:, size:]
    row_id = lax.broadcasted_iota(jnp.int32, (BLOCK, LANES), 0)
    for start in range(0, size, BLOCK):
        group = start // LANES
        lane = start % LANES
        panel = [
            m_ref[start : start + BLOCK, g * LANES : (g + 1) * LANES]
            for g in range(group, groups)
        ]
        head = panel[0]
        splat = [
            jnp.broadcast_to(head[:, lane + j : lane + j + 1], (BLOCK, LANES))
            for j in range(BLOCK)
        ]
        for j in range(BLOCK):
            inverse = 1.0 / splat[j][j : j + 1, :]
            at_pivot = row_id == j
            factor = splat[j]

            def step(block):
                scaled = block[j : j + 1, :] * inverse
                return jnp.where(at_pivot, scaled, block - factor * scaled)

            for later in range(j + 1, BLOCK):
                splat[later] = step(splat[later])
            panel = [step(block) for block in panel]
        top = jnp.concatenate(panel, axis=1)
        pieces = []
        if lane > 0:
            pieces.append(jnp.zeros((lane, top.shape[1]), jnp.float32))
        pieces.append(top)
        if lane + BLOCK < LANES:
            pieces.append(jnp.zeros((LANES - lane - BLOCK, top.shape[1]), jnp.float32))
        right = jnp.concatenate(pieces, axis=0)
        left = m_ref[:, group * LANES : (group + 1) * LANES]
        from_column = group * LANES
        after = start + BLOCK
        spans = []
        if after < size:
            spans.append((after, after + BLOCK))
            if after + BLOCK < size:
                spans.append((after + BLOCK, size))
        if start > 0:
            spans.append((0, start))
        for low, high in spans:
            m_ref[low:high, from_column:] = m_ref[low:high, from_column:] - exact_dot(
                left[low:high], right
            )
        m_ref[start:after, from_column:] = top
    w_ref[...] = m_ref[:, size:].astype(w_ref.dtype)


def solve_system(total):
    size = total.shape[0]
    whole = pl.BlockSpec(memory_space=pltpu.VMEM)
    return pl.pallas_call(
        solve_kernel,
        out_shape=jax.ShapeDtypeStruct((size, total.shape[1] - size), jnp.bfloat16),
        in_specs=[whole],
        out_specs=whole,
        scratch_shapes=[pltpu.VMEM(total.shape, jnp.float32)],
        compiler_params=pltpu.CompilerParams(vmem_limit_bytes=16 * 2**20),
        name="solve_system",
    )(total)


def body(
    predicted_moments,
    member_vectors,
    measured_moments,
    block_error_group,
    group_error_spread,
    background_spread,
    member_random_keys,
):
    devices_total = lax.axis_size("stat")
    stat_width = measured_moments.shape[0]
    total, closure, anomaly, params, spread = exchange(
        predicted_moments,
        member_vectors,
        measured_moments,
        block_error_group,
        group_error_spread,
        background_spread,
        member_random_keys,
        devices_total,
    )
    classes = group_error_spread.shape[0]
    selector = (block_error_group[:, None] == jnp.arange(classes, dtype=jnp.int32)[None, :]).astype(
        jnp.float32
    )
    slab_sigma = jnp.dot(selector, group_error_spread, precision=lax.Precision.HIGHEST)
    sigma = jnp.broadcast_to(slab_sigma[:, None], (block_error_group.shape[0], SLAB)).reshape(
        stat_width
    )
    weights = solve_system(total)
    updated_rows = (
        params.astype(jnp.float32) + transposed_product(weights, spread)
    ).astype(jnp.bfloat16)
    updated = lax.all_to_all(updated_rows, "stat", split_axis=0, concat_axis=1, tiled=True)
    predicted = (
        closure.astype(jnp.float32) + sigma[None, :] * transposed_product(weights, anomaly)
    ).astype(jnp.bfloat16)
    return (updated, predicted)


def solution(mesh):
    placed = (
        P(("groups", "stat"), None),
        P(("groups", "stat"), None),
        P(("groups", "stat")),
        P(("groups", "stat")),
        P("groups"),
        P("groups"),
        P("groups"),
    )
    return jax.shard_map(
        body,
        mesh=mesh,
        in_specs=placed,
        out_specs=(P(("groups", "stat"), None), P("groups", "stat")),
        check_vma=False,
    )
```

```python
import functools
import math

import jax
import jax.numpy as jnp
from jax import lax
from jax.experimental import pallas as pl
from jax.experimental.pallas import tpu as pltpu
from jax.sharding import PartitionSpec as P

SLAB = 512
LANES = 128
BLOCK = 16
MESH = pl.DeviceIdType.MESH

seed_factor = 668265261
index_factor = 374761393
scramble_one = 2146121005
scramble_two = 739982445


def scramble(hashed):
    hashed = hashed ^ lax.shift_right_logical(hashed, jnp.int32(16))
    hashed = hashed * scramble_one
    hashed = hashed ^ lax.shift_right_logical(hashed, jnp.int32(15))
    hashed = hashed * scramble_two
    return hashed ^ lax.shift_right_logical(hashed, jnp.int32(16))


def uniform_from(hashed):
    quotient = lax.shift_right_logical(scramble(hashed), jnp.int32(9))
    return (quotient.astype(jnp.float32) + 0.5) * 2.0 ** (-23)


def sine_of_turns(turns):
    square = turns * turns
    value = jnp.float32(0.0)
    for power in (11, 9, 7, 5, 3, 1):
        sign = -1.0 if power % 4 == 3 else 1.0
        value = value * square + sign * (2.0 * math.pi) ** power / math.factorial(power)
    return value * turns


def normal_from(hashed):
    first_part = uniform_from(hashed)
    second_part = uniform_from(hashed + 1)
    radius = jnp.sqrt(jnp.maximum(-2.0 * jnp.log(first_part), 0.0))
    return radius * sine_of_turns(jnp.abs(second_part - 0.5) - 0.25)


def inner(left, right):
    return lax.dot_general(
        left, right, (((1,), (1,)), ((), ())), preferred_element_type=jnp.float32
    )


def stages_of(mesh_size):
    rest = mesh_size // 2
    second = 1
    while second * second < rest:
        second *= 2
    return ((1, 2), (2, second), (2 * second, rest // second))


def signal_peers(barrier, me, devices_total):
    def signal(offset, carry):
        pl.semaphore_signal(
            barrier,
            inc=1,
            device_id={"stat": lax.rem(me + offset, devices_total)},
            device_id_type=MESH,
        )
        return carry

    lax.fori_loop(1, devices_total, signal, 0)


def sum_stages(stages, me, packed, recvs, totals, gathered, send_sem, recv_sem, gsend_sem, grecv_sem):
    count = len(stages)
    ways, chunks = packed.shape[:2]
    digits = [lax.rem(lax.div(me, stride), size) for stride, size in stages]
    lengths, bases, slots = [chunks], [0], [0]
    for t, (stride, size) in enumerate(stages):
        lengths.append(lengths[t] // size)
        bases.append(bases[t] + digits[t] * lengths[t + 1])
        slots.append(slots[t] + size - 1)

    def peer(t, offset):
        stride, size = stages[t]
        other = lax.rem(digits[t] + offset, size)
        return other, me + (other - digits[t]) * stride

    def source(t, way):
        return packed.at[way] if t == 0 else totals[t - 1].at[way]

    def start_scatter(t, way):
        copies = []
        for offset in range(1, stages[t][1]):
            other, device = peer(t, offset)
            slot = slots[t] + offset - 1
            copy = pltpu.make_async_remote_copy(
                src_ref=source(t, way).at[pl.ds(other * lengths[t + 1], lengths[t + 1])],
                dst_ref=recvs[t].at[way, offset - 1],
                send_sem=send_sem.at[way, slot],
                recv_sem=recv_sem.at[way, slot],
                device_id={"stat": device},
                device_id_type=MESH,
            )
            copy.start()
            copies.append(copy)
        return copies

    def start_gather(t, way):
        copies = []
        for offset in range(1, stages[t][1]):
            _, device = peer(t, offset)
            slot = slots[t] + offset - 1
            own = gathered.at[way, pl.ds(bases[t + 1], lengths[t + 1])]
            copy = pltpu.make_async_remote_copy(
                src_ref=own,
                dst_ref=own,
                send_sem=gsend_sem.at[way, slot],
                recv_sem=grecv_sem.at[way, slot],
                device_id={"stat": device},
                device_id_type=MESH,
            )
            copy.start()
            copies.append(copy)
        return copies

    flying = [start_scatter(0, way) for way in range(ways)]
    sent = []
    for t in range(count):
        for way in range(ways):
            copies = flying[way]
            value = source(t, way)[pl.ds(digits[t] * lengths[t + 1], lengths[t + 1])]
            for offset, copy in enumerate(copies):
                copy.wait_recv()
                value = value + recvs[t][way, offset]
            sent += copies
            if t + 1 < count:
                totals[t][way] = value
                flying[way] = start_scatter(t + 1, way)
            else:
                gathered[way, pl.ds(bases[count], lengths[count])] = value
                flying[way] = start_gather(t, way)
    for t in reversed(range(count)):
        for way in range(ways):
            for copy in flying[way]:
                copy.wait_recv()
            sent += flying[way]
            if t > 0:
                flying[way] = start_gather(t - 1, way)
    for copy in sent:
        copy.wait_send()


DRAW_ROWS = 8
DRAW_LANES = 1024
MIX = 13


def exchange_kernel(
    stages,
    devices_total,
    group_hbm,
    spread_of_group_hbm,
    prior_hbm,
    keys_hbm,
    measured_hbm,
    moments_ref,
    vectors_ref,
    total_ref,
    closure_hbm,
    anomaly_hbm,
    params_hbm,
    spread_hbm,
    group_ref,
    spread_of_group_ref,
    prior_ref,
    keys_row,
    keys_ref,
    measured_ref,
    got_moments,
    got_vectors,
    anomaly_ref,
    spread_ref,
    draws,
    part,
    packed,
    send_sem,
    recv_sem,
    own_sem,
    small_sem,
    out_sem,
    *sum_scratch,
):
    me = lax.axis_index("stat")
    members, stat_width = anomaly_ref.shape
    par_width = spread_ref.shape[1]
    root_scale = math.sqrt(members - 1.0)
    barrier = pltpu.get_barrier_semaphore()
    signal_peers(barrier, me, devices_total)
    small = []
    for index, (source, target) in enumerate(
        (
            (keys_hbm, keys_row),
            (measured_hbm, measured_ref),
            (group_hbm, group_ref),
            (spread_of_group_hbm, spread_of_group_ref),
            (prior_hbm, prior_ref),
        )
    ):
        copy = pltpu.make_async_copy(source, target, small_sem.at[index])
        copy.start()
        small.append(copy)
    pl.semaphore_wait(barrier, devices_total - 1)

    def columns(device, width):
        return pl.ds(pl.multiple_of(device * width, width), width)

    kinds = ((moments_ref, got_moments, stat_width), (vectors_ref, got_vectors, par_width))

    def copy_to(kind, step):
        source, slots, width = kinds[kind]
        device = lax.rem(me + lax.rem(step * MIX, devices_total), devices_total)
        return pltpu.make_async_remote_copy(
            src_ref=source.at[:, columns(device, width)],
            dst_ref=slots.at[me],
            send_sem=send_sem.at[kind, step],
            recv_sem=recv_sem.at[kind, step],
            device_id={"stat": device},
            device_id_type=MESH,
        )

    def copy_from(kind, step):
        source, slots, width = kinds[kind]
        device = lax.rem(
            me + devices_total - lax.rem(step * MIX, devices_total), devices_total
        )
        return pltpu.make_async_remote_copy(
            src_ref=source.at[:, columns(me, width)],
            dst_ref=slots.at[device],
            send_sem=send_sem.at[kind, step],
            recv_sem=recv_sem.at[kind, step],
            device_id={"stat": device},
            device_id_type=MESH,
        )

    own = []
    for kind, (source, slots, width) in enumerate(kinds):

        def start(step, carry, kind=kind):
            copy_to(kind, step).start()
            return carry

        lax.fori_loop(1, devices_total, start, 0)
        copy = pltpu.make_async_copy(
            source.at[:, columns(me, width)], slots.at[me], own_sem.at[kind]
        )
        copy.start()
        own.append(copy)

    def wait_kind(kind):
        def wait(step, carry):
            copy_from(kind, step).wait_recv()
            return carry

        lax.fori_loop(1, devices_total, wait, 0)
        own[kind].wait()

    for copy in small:
        copy.wait()
    for low in range(0, members, LANES):
        keys = jnp.broadcast_to(keys_row[:, low : low + LANES], (LANES, LANES))
        keys_ref[low : low + LANES, :] = keys.T * seed_factor
    lane = lax.broadcasted_iota(jnp.int32, (DRAW_ROWS, DRAW_LANES), 1)
    for first in range(0, stat_width + par_width, DRAW_LANES):
        if first < stat_width:
            position = me * stat_width + first
        else:
            position = devices_total * stat_width + me * par_width + (first - stat_width)
        offsets = (lane + position) * index_factor

        def draw(block, carry, first=first, offsets=offsets):
            rows = pl.ds(pl.multiple_of(block * DRAW_ROWS, DRAW_ROWS), DRAW_ROWS)
            seeds = jnp.concatenate([keys_ref[rows, :]] * (DRAW_LANES // LANES), axis=1)
            hashed = seeds + offsets
            draws[rows, first : first + DRAW_LANES] = normal_from(hashed)
            return carry

        lax.fori_loop(0, members // DRAW_ROWS, draw, 0)

    outgoing = []

    def send_out(source, target):
        copy = pltpu.make_async_copy(source, target, out_sem.at[len(outgoing)])
        copy.start()
        outgoing.append(copy)

    wait_kind(0)
    send_out(got_moments, closure_hbm)
    for slab in range(stat_width // SLAB):
        here = slice(slab * SLAB, (slab + 1) * SLAB)
        raw = got_moments[:, :, here].astype(jnp.float32).reshape(members, SLAB)
        sigma = jnp.full((1, SLAB), spread_of_group_ref[group_ref[slab]], jnp.float32)
        average = jnp.sum(raw, axis=0, keepdims=True) * (1.0 / members)
        anomaly = ((raw - average) * (1.0 / (sigma * root_scale))).astype(jnp.bfloat16)
        anomaly_ref[:, here] = anomaly
        misfit = (
            (measured_ref[:, here] - raw) * (1.0 / sigma) + draws[:, here]
        ).astype(jnp.bfloat16)
        product = inner(anomaly, jnp.concatenate([anomaly, misfit], axis=0))
        part[...] = product if slab == 0 else part[...] + product

    send_out(anomaly_ref, anomaly_hbm)
    wait_kind(1)
    send_out(got_vectors, params_hbm)
    prior = jnp.full((1, SLAB), prior_ref[0], jnp.float32)
    prior_inverse = 1.0 / prior
    lanes = lax.broadcasted_iota(jnp.int32, (1, 2 * members), 1)
    prior_members = jnp.full((1, 2 * members), prior_ref[0], jnp.float32)
    scale = 1.0 / jnp.where(lanes < members, prior_members * prior_members, prior_members)
    for slab in range(par_width // SLAB):
        here = slice(slab * SLAB, (slab + 1) * SLAB)
        raw = got_vectors[:, :, here].astype(jnp.float32).reshape(members, SLAB)
        average = jnp.sum(raw, axis=0, keepdims=True) * (1.0 / members)
        spread = ((raw - average) * (1.0 / root_scale)).astype(jnp.bfloat16)
        spread_ref[:, here] = spread
        drawn = draws[:, stat_width + slab * SLAB : stat_width + (slab + 1) * SLAB]
        misfit = (drawn - raw * prior_inverse).astype(jnp.bfloat16)
        product = inner(spread, jnp.concatenate([spread, misfit], axis=0))
        part[...] += product * scale

    send_out(spread_ref, spread_hbm)
    ways, chunks, _, width = packed.shape
    gathered = sum_scratch[2 * len(stages)]
    fold = (2 * members) // (width * ways)
    for way in range(ways):
        for side in range(fold):
            here = slice((way * fold + side) * width, (way * fold + side + 1) * width)
            block = part[:, here].reshape(members // 8, 8, width)
            if fold == 1:
                packed[way] = block
            else:
                for low in range(members // 8):
                    packed[way, low * fold + side] = block[low]
    sum_stages(
        stages,
        me,
        packed,
        sum_scratch[: len(stages)],
        sum_scratch[len(stages) : 2 * len(stages)],
        gathered,
        *sum_scratch[2 * len(stages) + 1 :],
    )
    for way in range(ways):
        for side in range(fold):
            here = slice((way * fold + side) * width, (way * fold + side + 1) * width)
            if fold == 1:
                total_ref[:, here] = gathered[way].reshape(members, width)
            else:
                for low in range(members // 8):
                    total_ref[low * 8 : low * 8 + 8, here] = gathered[way, low * fold + side]
    for copy in outgoing:
        copy.wait()

    def wait_sent(step, carry):
        copy_to(0, step).wait_send()
        copy_to(1, step).wait_send()
        return carry

    lax.fori_loop(1, devices_total, wait_sent, 0)


def exchange(
    predicted_moments,
    member_vectors,
    measured_moments,
    block_error_group,
    group_error_spread,
    background_spread,
    member_random_keys,
    devices_total,
):
    each, all_moments = predicted_moments.shape
    stat_width = all_moments // devices_total
    par_width = member_vectors.shape[1] // devices_total
    members = each * devices_total
    chunks = max(members // 8, devices_total)
    width = members // 8 * 2 * members // chunks
    ways = 2 if width == 2 * members else 1
    packed = (ways, chunks, 8, width // ways)
    stages = stages_of(devices_total)
    recvs, totals, length, copies = [], [], chunks, 0
    for stride, size in stages:
        length //= size
        recvs.append(pltpu.VMEM((ways, size - 1, length) + packed[2:], jnp.float32))
        totals.append(pltpu.VMEM((ways, length) + packed[2:], jnp.float32))
        copies += size - 1
    vmem = pl.BlockSpec(memory_space=pltpu.VMEM)
    hbm = pl.BlockSpec(memory_space=pltpu.HBM)
    shape = jax.ShapeDtypeStruct
    return pl.pallas_call(
        functools.partial(exchange_kernel, stages, devices_total),
        out_shape=(
            shape((members, 2 * members), jnp.float32),
            shape((devices_total, each, stat_width), jnp.bfloat16),
            shape((members, stat_width), jnp.bfloat16),
            shape((devices_total, each, par_width), jnp.bfloat16),
            shape((members, par_width), jnp.bfloat16),
        ),
        in_specs=[hbm] * 7,
        out_specs=(vmem, hbm, hbm, hbm, hbm),
        scratch_shapes=[
            pltpu.SMEM(block_error_group.shape, jnp.int32),
            pltpu.SMEM(group_error_spread.shape, jnp.float32),
            pltpu.SMEM(background_spread.shape, jnp.float32),
            pltpu.VMEM((1, members), jnp.int32),
            pltpu.VMEM((members, LANES), jnp.int32),
            pltpu.VMEM((1, stat_width), jnp.float32),
            pltpu.VMEM((devices_total, each, stat_width), jnp.bfloat16),
            pltpu.VMEM((devices_total, each, par_width), jnp.bfloat16),
            pltpu.VMEM((members, stat_width), jnp.bfloat16),
            pltpu.VMEM((members, par_width), jnp.bfloat16),
            pltpu.VMEM((members, stat_width + par_width), jnp.float32),
            pltpu.VMEM((members, 2 * members), jnp.float32),
            pltpu.VMEM(packed, jnp.float32),
            pltpu.SemaphoreType.DMA((2, devices_total)),
            pltpu.SemaphoreType.DMA((2, devices_total)),
            pltpu.SemaphoreType.DMA((2,)),
            pltpu.SemaphoreType.DMA((5,)),
            pltpu.SemaphoreType.DMA((4,)),
        ]
        + recvs
        + totals
        + [pltpu.VMEM(packed, jnp.float32)]
        + [pltpu.SemaphoreType.DMA((ways, copies))] * 4,
        compiler_params=pltpu.CompilerParams(
            collective_id=0, has_side_effects=True, vmem_limit_bytes=40 * 2**20
        ),
        name="exchange",
    )(
        block_error_group,
        group_error_spread,
        background_spread,
        member_random_keys[None, :],
        measured_moments[None, :],
        predicted_moments,
        member_vectors,
    )


def exact_dot(left, right):
    return jnp.dot(
        left, right, preferred_element_type=jnp.float32, precision=lax.Precision.HIGHEST
    )


def solve_kernel(s_ref, w_ref, m_ref):
    size = s_ref.shape[0]
    groups = s_ref.shape[1] // LANES
    own = size // LANES
    row = lax.broadcasted_iota(jnp.int32, (size, size), 0)
    column = lax.broadcasted_iota(jnp.int32, (size, size), 1)
    m_ref[:, :size] = s_ref[:, :size] + (row == column).astype(jnp.float32)
    m_ref[:, size:] = s_ref[:, size:]
    row_id = lax.broadcasted_iota(jnp.int32, (BLOCK, LANES), 0)
    for start in range(0, size, BLOCK):
        group = start // LANES
        lane = start % LANES
        panel = [
            m_ref[start : start + BLOCK, g * LANES : (g + 1) * LANES]
            for g in range(group, groups)
        ]
        head = panel[0]
        splat = [
            jnp.broadcast_to(head[:, lane + j : lane + j + 1], (BLOCK, LANES))
            for j in range(BLOCK)
        ]
        for j in range(BLOCK):
            inverse = 1.0 / splat[j][j : j + 1, :]
            at_pivot = row_id == j
            factor = splat[j]

            def step(block):
                scaled = block[j : j + 1, :] * inverse
                return jnp.where(at_pivot, scaled, block - factor * scaled)

            for later in range(j + 1, BLOCK):
                splat[later] = step(splat[later])
            panel = [step(block) for block in panel]
        top = jnp.concatenate(panel, axis=1)
        pieces = []
        if lane > 0:
            pieces.append(jnp.zeros((lane, top.shape[1]), jnp.float32))
        pieces.append(top)
        if lane + BLOCK < LANES:
            pieces.append(jnp.zeros((LANES - lane - BLOCK, top.shape[1]), jnp.float32))
        right = jnp.concatenate(pieces, axis=0)
        left = m_ref[:, group * LANES : (group + 1) * LANES]
        from_column = group * LANES
        after = start + BLOCK
        spans = []
        if after < size:
            spans.append((after, after + BLOCK))
            if after + BLOCK < size:
                spans.append((after + BLOCK, size))
        if start > 0:
            spans.append((0, start))
        for low, high in spans:
            m_ref[low:high, from_column:] = m_ref[low:high, from_column:] - exact_dot(
                left[low:high], right
            )
        m_ref[start:after, from_column:] = top
    w_ref[...] = m_ref[:, size:].T.astype(w_ref.dtype)


def solve_system(total):
    size = total.shape[0]
    whole = pl.BlockSpec(memory_space=pltpu.VMEM)
    return pl.pallas_call(
        solve_kernel,
        out_shape=jax.ShapeDtypeStruct((size, total.shape[1] - size), jnp.bfloat16),
        in_specs=[whole],
        out_specs=whole,
        scratch_shapes=[pltpu.VMEM(total.shape, jnp.float32)],
        compiler_params=pltpu.CompilerParams(vmem_limit_bytes=16 * 2**20),
        name="solve_system",
    )(total)


def update_kernel(
    devices_total,
    group_ref,
    spread_of_group_ref,
    weights_ref,
    closure_ref,
    anomaly_ref,
    params_ref,
    spread_ref,
    updated_ref,
    predicted_ref,
    rows,
    send_sem,
    recv_sem,
    own_sem,
):
    me = lax.axis_index("stat")
    each, par_width = rows.shape[1:]
    members, stat_width = anomaly_ref.shape
    barrier = pltpu.get_barrier_semaphore()
    signal_peers(barrier, me, devices_total)
    weights = weights_ref[...]
    for low in range(0, par_width, SLAB):
        here = slice(low, low + SLAB)
        change = jnp.dot(weights, spread_ref[:, here], preferred_element_type=jnp.float32)
        new = params_ref[:, :, here].astype(jnp.float32) + change.reshape(devices_total, each, SLAB)
        rows[:, :, here] = new.astype(jnp.bfloat16)
    pl.semaphore_wait(barrier, devices_total - 1)

    def columns(device):
        return pl.ds(pl.multiple_of(device * par_width, par_width), par_width)

    def copy_to(step, owner):
        device = lax.rem(me + lax.rem(step * MIX, devices_total), devices_total)
        if owner is None:
            owner = lax.rem(
                me + devices_total - lax.rem(step * MIX, devices_total), devices_total
            )
        return pltpu.make_async_remote_copy(
            src_ref=rows.at[device],
            dst_ref=updated_ref.at[:, columns(owner)],
            send_sem=send_sem.at[step],
            recv_sem=recv_sem.at[step],
            device_id={"stat": device},
            device_id_type=MESH,
        )

    def start(step, carry):
        copy_to(step, me).start()
        return carry

    lax.fori_loop(1, devices_total, start, 0)
    own = pltpu.make_async_copy(rows.at[me], updated_ref.at[:, columns(me)], own_sem)
    own.start()
    for slab in range(stat_width // SLAB):
        here = slice(slab * SLAB, (slab + 1) * SLAB)
        change = jnp.dot(weights, anomaly_ref[:, here], preferred_element_type=jnp.float32)
        sigma = jnp.full((1, SLAB), spread_of_group_ref[group_ref[slab]], jnp.float32)
        raw = closure_ref[:, :, here].astype(jnp.float32).reshape(members, SLAB)
        predicted_ref[:, here] = (raw + sigma * change).astype(jnp.bfloat16)

    def finish(step, carry):
        copy_to(step, None).wait_recv()
        copy_to(step, me).wait_send()
        return carry

    lax.fori_loop(1, devices_total, finish, 0)
    own.wait()


def update(
    block_error_group, group_error_spread, weights, closure, anomaly, params, spread
):
    devices_total, each, par_width = params.shape
    vmem = pl.BlockSpec(memory_space=pltpu.VMEM)
    smem = pl.BlockSpec(memory_space=pltpu.SMEM)
    return pl.pallas_call(
        functools.partial(update_kernel, devices_total),
        out_shape=(
            jax.ShapeDtypeStruct((each, devices_total * par_width), jnp.bfloat16),
            jax.ShapeDtypeStruct(anomaly.shape, jnp.bfloat16),
        ),
        in_specs=[smem, smem] + [vmem] * 5,
        out_specs=(vmem, vmem),
        scratch_shapes=[
            pltpu.VMEM(params.shape, jnp.bfloat16),
            pltpu.SemaphoreType.DMA((devices_total,)),
            pltpu.SemaphoreType.DMA((devices_total,)),
            pltpu.SemaphoreType.DMA,
        ],
        compiler_params=pltpu.CompilerParams(
            collective_id=1, has_side_effects=True, vmem_limit_bytes=24 * 2**20
        ),
        name="update",
    )(block_error_group, group_error_spread, weights, closure, anomaly, params, spread)


def body(
    predicted_moments,
    member_vectors,
    measured_moments,
    block_error_group,
    group_error_spread,
    background_spread,
    member_random_keys,
):
    total, closure, anomaly, params, spread = exchange(
        predicted_moments,
        member_vectors,
        measured_moments,
        block_error_group,
        group_error_spread,
        background_spread,
        member_random_keys,
        lax.axis_size("stat"),
    )
    weights = solve_system(total)
    return update(
        block_error_group, group_error_spread, weights, closure, anomaly, params, spread
    )


def solution(mesh):
    placed = (
        P(("groups", "stat"), None),
        P(("groups", "stat"), None),
        P(("groups", "stat")),
        P(("groups", "stat")),
        P("groups"),
        P("groups"),
        P("groups"),
    )
    return jax.shard_map(
        body,
        mesh=mesh,
        in_specs=placed,
        out_specs=(P(("groups", "stat"), None), P("groups", "stat")),
        check_vma=False,
    )
```

```python
import functools
import math

import jax
import jax.numpy as jnp
from jax import lax
from jax.experimental import pallas as pl
from jax.experimental.pallas import tpu as pltpu
from jax.sharding import PartitionSpec as P

SLAB = 512
LANES = 128
BLOCK = 16
MESH = pl.DeviceIdType.MESH

seed_factor = 668265261
index_factor = 374761393
scramble_one = 2146121005
scramble_two = 739982445


def scramble(hashed):
    hashed = hashed ^ lax.shift_right_logical(hashed, jnp.int32(16))
    hashed = hashed * scramble_one
    hashed = hashed ^ lax.shift_right_logical(hashed, jnp.int32(15))
    hashed = hashed * scramble_two
    return hashed ^ lax.shift_right_logical(hashed, jnp.int32(16))


def uniform_from(hashed):
    quotient = lax.shift_right_logical(scramble(hashed), jnp.int32(9))
    return (quotient.astype(jnp.float32) + 0.5) * 2.0 ** (-23)


def sine_of_turns(turns):
    square = turns * turns
    value = jnp.float32(0.0)
    for power in (11, 9, 7, 5, 3, 1):
        sign = -1.0 if power % 4 == 3 else 1.0
        value = value * square + sign * (2.0 * math.pi) ** power / math.factorial(power)
    return value * turns


def normal_from(hashed):
    first_part = uniform_from(hashed)
    second_part = uniform_from(hashed + 1)
    radius = jnp.sqrt(jnp.maximum(-2.0 * jnp.log(first_part), 0.0))
    return radius * sine_of_turns(jnp.abs(second_part - 0.5) - 0.25)


def inner(left, right):
    return lax.dot_general(
        left, right, (((1,), (1,)), ((), ())), preferred_element_type=jnp.float32
    )


def stages_of(mesh_size):
    rest = mesh_size // 2
    second = 1
    while second * second < rest:
        second *= 2
    return ((1, 2), (2, second), (2 * second, rest // second))


def signal_peers(barrier, me, devices_total):
    def signal(offset, carry):
        pl.semaphore_signal(
            barrier,
            inc=1,
            device_id={"stat": lax.rem(me + offset, devices_total)},
            device_id_type=MESH,
        )
        return carry

    lax.fori_loop(1, devices_total, signal, 0)


def sum_stages(stages, me, packed, recvs, totals, gathered, send_sem, recv_sem, gsend_sem, grecv_sem):
    count = len(stages)
    ways, chunks = packed.shape[:2]
    digits = [lax.rem(lax.div(me, stride), size) for stride, size in stages]
    lengths, bases, slots = [chunks], [0], [0]
    for t, (stride, size) in enumerate(stages):
        lengths.append(lengths[t] // size)
        bases.append(bases[t] + digits[t] * lengths[t + 1])
        slots.append(slots[t] + size - 1)

    def peer(t, offset):
        stride, size = stages[t]
        other = lax.rem(digits[t] + offset, size)
        return other, me + (other - digits[t]) * stride

    def source(t, way):
        return packed.at[way] if t == 0 else totals[t - 1].at[way]

    def start_scatter(t, way):
        copies = []
        for offset in range(1, stages[t][1]):
            other, device = peer(t, offset)
            slot = slots[t] + offset - 1
            copy = pltpu.make_async_remote_copy(
                src_ref=source(t, way).at[pl.ds(other * lengths[t + 1], lengths[t + 1])],
                dst_ref=recvs[t].at[way, offset - 1],
                send_sem=send_sem.at[way, slot],
                recv_sem=recv_sem.at[way, slot],
                device_id={"stat": device},
                device_id_type=MESH,
            )
            copy.start()
            copies.append(copy)
        return copies

    def start_gather(t, way):
        copies = []
        for offset in range(1, stages[t][1]):
            _, device = peer(t, offset)
            slot = slots[t] + offset - 1
            own = gathered.at[way, pl.ds(bases[t + 1], lengths[t + 1])]
            copy = pltpu.make_async_remote_copy(
                src_ref=own,
                dst_ref=own,
                send_sem=gsend_sem.at[way, slot],
                recv_sem=grecv_sem.at[way, slot],
                device_id={"stat": device},
                device_id_type=MESH,
            )
            copy.start()
            copies.append(copy)
        return copies

    flying = [start_scatter(0, way) for way in range(ways)]
    sent = []
    for t in range(count):
        for way in range(ways):
            copies = flying[way]
            value = source(t, way)[pl.ds(digits[t] * lengths[t + 1], lengths[t + 1])]
            for offset, copy in enumerate(copies):
                copy.wait_recv()
                value = value + recvs[t][way, offset]
            sent += copies
            if t + 1 < count:
                totals[t][way] = value
                flying[way] = start_scatter(t + 1, way)
            else:
                gathered[way, pl.ds(bases[count], lengths[count])] = value
                flying[way] = start_gather(t, way)
    for t in reversed(range(count)):
        for way in range(ways):
            for copy in flying[way]:
                copy.wait_recv()
            sent += flying[way]
            if t > 0:
                flying[way] = start_gather(t - 1, way)
    for copy in sent:
        copy.wait_send()


DRAW_ROWS = 8
DRAW_LANES = 1024
MIX = 1


def exchange_kernel(
    stages,
    devices_total,
    group_hbm,
    spread_of_group_hbm,
    prior_hbm,
    keys_hbm,
    measured_hbm,
    moments_ref,
    vectors_ref,
    total_ref,
    closure_hbm,
    anomaly_hbm,
    params_hbm,
    spread_hbm,
    group_ref,
    spread_of_group_ref,
    prior_ref,
    keys_row,
    keys_ref,
    measured_ref,
    got_moments,
    got_vectors,
    anomaly_ref,
    spread_ref,
    draws,
    part,
    packed,
    send_sem,
    recv_sem,
    own_sem,
    small_sem,
    out_sem,
    *sum_scratch,
):
    me = lax.axis_index("stat")
    members, stat_width = anomaly_ref.shape
    par_width = spread_ref.shape[1]
    root_scale = math.sqrt(members - 1.0)
    barrier = pltpu.get_barrier_semaphore()
    signal_peers(barrier, me, devices_total)
    small = []
    for index, (source, target) in enumerate(
        (
            (keys_hbm, keys_row),
            (measured_hbm, measured_ref),
            (group_hbm, group_ref),
            (spread_of_group_hbm, spread_of_group_ref),
            (prior_hbm, prior_ref),
        )
    ):
        copy = pltpu.make_async_copy(source, target, small_sem.at[index])
        copy.start()
        small.append(copy)
    pl.semaphore_wait(barrier, devices_total - 1)

    def columns(device, width):
        return pl.ds(pl.multiple_of(device * width, width), width)

    kinds = ((moments_ref, got_moments, stat_width), (vectors_ref, got_vectors, par_width))

    def copy_to(kind, step):
        source, slots, width = kinds[kind]
        device = lax.rem(me + lax.rem(step * MIX, devices_total), devices_total)
        return pltpu.make_async_remote_copy(
            src_ref=source.at[:, columns(device, width)],
            dst_ref=slots.at[me],
            send_sem=send_sem.at[kind, step],
            recv_sem=recv_sem.at[kind, step],
            device_id={"stat": device},
            device_id_type=MESH,
        )

    def copy_from(kind, step):
        source, slots, width = kinds[kind]
        device = lax.rem(
            me + devices_total - lax.rem(step * MIX, devices_total), devices_total
        )
        return pltpu.make_async_remote_copy(
            src_ref=source.at[:, columns(me, width)],
            dst_ref=slots.at[device],
            send_sem=send_sem.at[kind, step],
            recv_sem=recv_sem.at[kind, step],
            device_id={"stat": device},
            device_id_type=MESH,
        )

    own = []
    for kind, (source, slots, width) in enumerate(kinds):

        def start(step, carry, kind=kind):
            copy_to(kind, step).start()
            return carry

        lax.fori_loop(1, devices_total, start, 0)
        copy = pltpu.make_async_copy(
            source.at[:, columns(me, width)], slots.at[me], own_sem.at[kind]
        )
        copy.start()
        own.append(copy)

    def wait_kind(kind):
        def wait(step, carry):
            copy_from(kind, step).wait_recv()
            return carry

        lax.fori_loop(1, devices_total, wait, 0)
        own[kind].wait()

    for copy in small:
        copy.wait()
    for low in range(0, members, LANES):
        keys = jnp.broadcast_to(keys_row[:, low : low + LANES], (LANES, LANES))
        keys_ref[low : low + LANES, :] = keys.T * seed_factor
    lane = lax.broadcasted_iota(jnp.int32, (DRAW_ROWS, DRAW_LANES), 1)
    for first in range(0, stat_width + par_width, DRAW_LANES):
        if first < stat_width:
            position = me * stat_width + first
        else:
            position = devices_total * stat_width + me * par_width + (first - stat_width)
        offsets = (lane + position) * index_factor

        def draw(block, carry, first=first, offsets=offsets):
            rows = pl.ds(pl.multiple_of(block * DRAW_ROWS, DRAW_ROWS), DRAW_ROWS)
            seeds = jnp.concatenate([keys_ref[rows, :]] * (DRAW_LANES // LANES), axis=1)
            hashed = seeds + offsets
            draws[rows, first : first + DRAW_LANES] = normal_from(hashed)
            return carry

        lax.fori_loop(0, members // DRAW_ROWS, draw, 0)

    outgoing = []

    def send_out(source, target):
        copy = pltpu.make_async_copy(source, target, out_sem.at[len(outgoing)])
        copy.start()
        outgoing.append(copy)

    wait_kind(0)
    send_out(got_moments, closure_hbm)
    for slab in range(stat_width // SLAB):
        here = slice(slab * SLAB, (slab + 1) * SLAB)
        raw = got_moments[:, :, here].astype(jnp.float32).reshape(members, SLAB)
        sigma = jnp.full((1, SLAB), spread_of_group_ref[group_ref[slab]], jnp.float32)
        average = jnp.sum(raw, axis=0, keepdims=True) * (1.0 / members)
        anomaly = ((raw - average) * (1.0 / (sigma * root_scale))).astype(jnp.bfloat16)
        anomaly_ref[:, here] = anomaly
        misfit = (
            (measured_ref[:, here] - raw) * (1.0 / sigma) + draws[:, here]
        ).astype(jnp.bfloat16)
        product = inner(anomaly, jnp.concatenate([anomaly, misfit], axis=0))
        part[...] = product if slab == 0 else part[...] + product

    send_out(anomaly_ref, anomaly_hbm)
    wait_kind(1)
    send_out(got_vectors, params_hbm)
    prior = jnp.full((1, SLAB), prior_ref[0], jnp.float32)
    prior_inverse = 1.0 / prior
    lanes = lax.broadcasted_iota(jnp.int32, (1, 2 * members), 1)
    prior_members = jnp.full((1, 2 * members), prior_ref[0], jnp.float32)
    scale = 1.0 / jnp.where(lanes < members, prior_members * prior_members, prior_members)
    for slab in range(par_width // SLAB):
        here = slice(slab * SLAB, (slab + 1) * SLAB)
        raw = got_vectors[:, :, here].astype(jnp.float32).reshape(members, SLAB)
        average = jnp.sum(raw, axis=0, keepdims=True) * (1.0 / members)
        spread = ((raw - average) * (1.0 / root_scale)).astype(jnp.bfloat16)
        spread_ref[:, here] = spread
        drawn = draws[:, stat_width + slab * SLAB : stat_width + (slab + 1) * SLAB]
        misfit = (drawn - raw * prior_inverse).astype(jnp.bfloat16)
        product = inner(spread, jnp.concatenate([spread, misfit], axis=0))
        part[...] += product * scale

    send_out(spread_ref, spread_hbm)
    ways, chunks, _, width = packed.shape
    gathered = sum_scratch[2 * len(stages)]
    fold = (2 * members) // (width * ways)
    for way in range(ways):
        for side in range(fold):
            here = slice((way * fold + side) * width, (way * fold + side + 1) * width)
            block = part[:, here].reshape(members // 8, 8, width)
            if fold == 1:
                packed[way] = block
            else:
                for low in range(members // 8):
                    packed[way, low * fold + side] = block[low]
    sum_stages(
        stages,
        me,
        packed,
        sum_scratch[: len(stages)],
        sum_scratch[len(stages) : 2 * len(stages)],
        gathered,
        *sum_scratch[2 * len(stages) + 1 :],
    )
    for way in range(ways):
        for side in range(fold):
            here = slice((way * fold + side) * width, (way * fold + side + 1) * width)
            if fold == 1:
                total_ref[:, here] = gathered[way].reshape(members, width)
            else:
                for low in range(members // 8):
                    total_ref[low * 8 : low * 8 + 8, here] = gathered[way, low * fold + side]
    for copy in outgoing:
        copy.wait()

    def wait_sent(step, carry):
        copy_to(0, step).wait_send()
        copy_to(1, step).wait_send()
        return carry

    lax.fori_loop(1, devices_total, wait_sent, 0)


def exchange(
    predicted_moments,
    member_vectors,
    measured_moments,
    block_error_group,
    group_error_spread,
    background_spread,
    member_random_keys,
    devices_total,
):
    each, all_moments = predicted_moments.shape
    stat_width = all_moments // devices_total
    par_width = member_vectors.shape[1] // devices_total
    members = each * devices_total
    chunks = max(members // 8, devices_total)
    width = members // 8 * 2 * members // chunks
    ways = 2 if width == 2 * members else 1
    packed = (ways, chunks, 8, width // ways)
    stages = stages_of(devices_total)
    recvs, totals, length, copies = [], [], chunks, 0
    for stride, size in stages:
        length //= size
        recvs.append(pltpu.VMEM((ways, size - 1, length) + packed[2:], jnp.float32))
        totals.append(pltpu.VMEM((ways, length) + packed[2:], jnp.float32))
        copies += size - 1
    vmem = pl.BlockSpec(memory_space=pltpu.VMEM)
    hbm = pl.BlockSpec(memory_space=pltpu.HBM)
    shape = jax.ShapeDtypeStruct
    return pl.pallas_call(
        functools.partial(exchange_kernel, stages, devices_total),
        out_shape=(
            shape((members, 2 * members), jnp.float32),
            shape((devices_total, each, stat_width), jnp.bfloat16),
            shape((members, stat_width), jnp.bfloat16),
            shape((devices_total, each, par_width), jnp.bfloat16),
            shape((members, par_width), jnp.bfloat16),
        ),
        in_specs=[hbm] * 7,
        out_specs=(vmem, hbm, hbm, hbm, hbm),
        scratch_shapes=[
            pltpu.SMEM(block_error_group.shape, jnp.int32),
            pltpu.SMEM(group_error_spread.shape, jnp.float32),
            pltpu.SMEM(background_spread.shape, jnp.float32),
            pltpu.VMEM((1, members), jnp.int32),
            pltpu.VMEM((members, LANES), jnp.int32),
            pltpu.VMEM((1, stat_width), jnp.float32),
            pltpu.VMEM((devices_total, each, stat_width), jnp.bfloat16),
            pltpu.VMEM((devices_total, each, par_width), jnp.bfloat16),
            pltpu.VMEM((members, stat_width), jnp.bfloat16),
            pltpu.VMEM((members, par_width), jnp.bfloat16),
            pltpu.VMEM((members, stat_width + par_width), jnp.float32),
            pltpu.VMEM((members, 2 * members), jnp.float32),
            pltpu.VMEM(packed, jnp.float32),
            pltpu.SemaphoreType.DMA((2, devices_total)),
            pltpu.SemaphoreType.DMA((2, devices_total)),
            pltpu.SemaphoreType.DMA((2,)),
            pltpu.SemaphoreType.DMA((5,)),
            pltpu.SemaphoreType.DMA((4,)),
        ]
        + recvs
        + totals
        + [pltpu.VMEM(packed, jnp.float32)]
        + [pltpu.SemaphoreType.DMA((ways, copies))] * 4,
        compiler_params=pltpu.CompilerParams(
            collective_id=0, has_side_effects=True, vmem_limit_bytes=40 * 2**20
        ),
        name="exchange",
    )(
        block_error_group,
        group_error_spread,
        background_spread,
        member_random_keys[None, :],
        measured_moments[None, :],
        predicted_moments,
        member_vectors,
    )


def exact_dot(left, right):
    return jnp.dot(
        left, right, preferred_element_type=jnp.float32, precision=lax.Precision.HIGHEST
    )


def solve_kernel(s_ref, w_ref, m_ref):
    size = s_ref.shape[0]
    groups = s_ref.shape[1] // LANES
    own = size // LANES
    row = lax.broadcasted_iota(jnp.int32, (size, size), 0)
    column = lax.broadcasted_iota(jnp.int32, (size, size), 1)
    m_ref[:, :size] = s_ref[:, :size] + (row == column).astype(jnp.float32)
    m_ref[:, size:] = s_ref[:, size:]
    row_id = lax.broadcasted_iota(jnp.int32, (BLOCK, LANES), 0)
    for start in range(0, size, BLOCK):
        group = start // LANES
        lane = start % LANES
        panel = [
            m_ref[start : start + BLOCK, g * LANES : (g + 1) * LANES]
            for g in range(group, groups)
        ]
        head = panel[0]
        splat = [
            jnp.broadcast_to(head[:, lane + j : lane + j + 1], (BLOCK, LANES))
            for j in range(BLOCK)
        ]
        for j in range(BLOCK):
            inverse = 1.0 / splat[j][j : j + 1, :]
            at_pivot = row_id == j
            factor = splat[j]

            def step(block):
                scaled = block[j : j + 1, :] * inverse
                return jnp.where(at_pivot, scaled, block - factor * scaled)

            for later in range(j + 1, BLOCK):
                splat[later] = step(splat[later])
            panel = [step(block) for block in panel]
        top = jnp.concatenate(panel, axis=1)
        pieces = []
        if lane > 0:
            pieces.append(jnp.zeros((lane, top.shape[1]), jnp.float32))
        pieces.append(top)
        if lane + BLOCK < LANES:
            pieces.append(jnp.zeros((LANES - lane - BLOCK, top.shape[1]), jnp.float32))
        right = jnp.concatenate(pieces, axis=0)
        left = m_ref[:, group * LANES : (group + 1) * LANES]
        from_column = group * LANES
        after = start + BLOCK
        spans = []
        if after < size:
            spans.append((after, after + BLOCK))
            if after + BLOCK < size:
                spans.append((after + BLOCK, size))
        if start > 0:
            spans.append((0, start))
        for low, high in spans:
            m_ref[low:high, from_column:] = m_ref[low:high, from_column:] - exact_dot(
                left[low:high], right
            )
        m_ref[start:after, from_column:] = top
    w_ref[...] = m_ref[:, size:].T.astype(w_ref.dtype)


def solve_system(total):
    size = total.shape[0]
    whole = pl.BlockSpec(memory_space=pltpu.VMEM)
    return pl.pallas_call(
        solve_kernel,
        out_shape=jax.ShapeDtypeStruct((size, total.shape[1] - size), jnp.bfloat16),
        in_specs=[whole],
        out_specs=whole,
        scratch_shapes=[pltpu.VMEM(total.shape, jnp.float32)],
        compiler_params=pltpu.CompilerParams(vmem_limit_bytes=16 * 2**20),
        name="solve_system",
    )(total)


def update_kernel(
    devices_total,
    group_ref,
    spread_of_group_ref,
    weights_ref,
    closure_ref,
    anomaly_ref,
    params_ref,
    spread_ref,
    updated_ref,
    predicted_ref,
    rows,
    send_sem,
    recv_sem,
    own_sem,
):
    me = lax.axis_index("stat")
    each, par_width = rows.shape[1:]
    members, stat_width = anomaly_ref.shape
    barrier = pltpu.get_barrier_semaphore()
    signal_peers(barrier, me, devices_total)
    weights = weights_ref[...]
    for low in range(0, par_width, SLAB):
        here = slice(low, low + SLAB)
        change = jnp.dot(weights, spread_ref[:, here], preferred_element_type=jnp.float32)
        new = params_ref[:, :, here].astype(jnp.float32) + change.reshape(devices_total, each, SLAB)
        rows[:, :, here] = new.astype(jnp.bfloat16)
    pl.semaphore_wait(barrier, devices_total - 1)

    def columns(device):
        return pl.ds(pl.multiple_of(device * par_width, par_width), par_width)

    def copy_to(step, owner):
        device = lax.rem(me + lax.rem(step * MIX, devices_total), devices_total)
        if owner is None:
            owner = lax.rem(
                me + devices_total - lax.rem(step * MIX, devices_total), devices_total
            )
        return pltpu.make_async_remote_copy(
            src_ref=rows.at[device],
            dst_ref=updated_ref.at[:, columns(owner)],
            send_sem=send_sem.at[step],
            recv_sem=recv_sem.at[step],
            device_id={"stat": device},
            device_id_type=MESH,
        )

    def start(step, carry):
        copy_to(step, me).start()
        return carry

    lax.fori_loop(1, devices_total, start, 0)
    own = pltpu.make_async_copy(rows.at[me], updated_ref.at[:, columns(me)], own_sem)
    own.start()
    for slab in range(stat_width // SLAB):
        here = slice(slab * SLAB, (slab + 1) * SLAB)
        change = jnp.dot(weights, anomaly_ref[:, here], preferred_element_type=jnp.float32)
        sigma = jnp.full((1, SLAB), spread_of_group_ref[group_ref[slab]], jnp.float32)
        raw = closure_ref[:, :, here].astype(jnp.float32).reshape(members, SLAB)
        predicted_ref[:, here] = (raw + sigma * change).astype(jnp.bfloat16)

    def finish(step, carry):
        copy_to(step, None).wait_recv()
        copy_to(step, me).wait_send()
        return carry

    lax.fori_loop(1, devices_total, finish, 0)
    own.wait()


def update(
    block_error_group, group_error_spread, weights, closure, anomaly, params, spread
):
    devices_total, each, par_width = params.shape
    vmem = pl.BlockSpec(memory_space=pltpu.VMEM)
    smem = pl.BlockSpec(memory_space=pltpu.SMEM)
    return pl.pallas_call(
        functools.partial(update_kernel, devices_total),
        out_shape=(
            jax.ShapeDtypeStruct((each, devices_total * par_width), jnp.bfloat16),
            jax.ShapeDtypeStruct(anomaly.shape, jnp.bfloat16),
        ),
        in_specs=[smem, smem] + [vmem] * 5,
        out_specs=(vmem, vmem),
        scratch_shapes=[
            pltpu.VMEM(params.shape, jnp.bfloat16),
            pltpu.SemaphoreType.DMA((devices_total,)),
            pltpu.SemaphoreType.DMA((devices_total,)),
            pltpu.SemaphoreType.DMA,
        ],
        compiler_params=pltpu.CompilerParams(
            collective_id=1, has_side_effects=True, vmem_limit_bytes=24 * 2**20
        ),
        name="update",
    )(block_error_group, group_error_spread, weights, closure, anomaly, params, spread)


def body(
    predicted_moments,
    member_vectors,
    measured_moments,
    block_error_group,
    group_error_spread,
    background_spread,
    member_random_keys,
):
    total, closure, anomaly, params, spread = exchange(
        predicted_moments,
        member_vectors,
        measured_moments,
        block_error_group,
        group_error_spread,
        background_spread,
        member_random_keys,
        lax.axis_size("stat"),
    )
    weights = solve_system(total)
    return update(
        block_error_group, group_error_spread, weights, closure, anomaly, params, spread
    )


def solution(mesh):
    placed = (
        P(("groups", "stat"), None),
        P(("groups", "stat"), None),
        P(("groups", "stat")),
        P(("groups", "stat")),
        P("groups"),
        P("groups"),
        P("groups"),
    )
    return jax.shard_map(
        body,
        mesh=mesh,
        in_specs=placed,
        out_specs=(P(("groups", "stat"), None), P("groups", "stat")),
        check_vma=False,
    )
```
